32 devices in a mesh: groups: 2 (over y), space: 4 (over x, core), chan: 4 (over z).
Axes of the slice: x: 2, y: 2, z: 4, core: 2. Of those that a mesh axis runs over, the one named last changes fastest.
Arguments:
- fields: bfloat16 [1024, 16, 256], P('chan', ('groups', 'space')), parts along dimension 1, may hold values from -6 to 6
- conv_weight: bfloat16 [27, 1024, 1024], P(None, 'chan', 'space'), may hold values from -0.0390625 to 0.0390625
Outputs:
- convolved: bfloat16 [1024, 16, 256], P('chan', ('groups', 'space')), parts along dimension 1
The draws below stay inside these ranges and needn't reach their ends.
There are 2 independent parts, one for each index of `groups`. The reference program is written for one: setup_inputs(seed, part) draws one part's arguments, and reference() takes and returns one part's arrays. A program takes and returns all parts, laid end to end along the dimension named above; an argument that names none is the same for every part. Nothing has to cross between parts.
All inputs are finite; a program needn't handle non-finite values.
Results may differ from the reference program's by a relative error of at most 0.001.
Values may be sent and summed in bfloat16 or wider, within the bound.
No kernel may reach another device: no remote copies, remote signals or barrier semaphores. Data moves between devices by JAX's collectives and lax.ppermute only.
A program may use at most 128 MiB of HBM per device.

```python
import jax
import jax.numpy as jnp
from jax import lax

C = 1024
NY = 16
NZ = 16
NX = 8


def block_levels(own_key, dims, cuts, low, top_value):
    loudness, own = 1.0, jax.random.fold_in(own_key, 6)
    for dim, blocks in cuts:
        heights = jnp.exp(jax.random.uniform(jax.random.fold_in(own, dim), (blocks,), jnp.float32, low / len(cuts), top_value / len(cuts)))
        loudness = loudness * jnp.repeat(heights, dims[dim] // blocks).reshape([-1 if axis == dim else 1 for axis in range(len(dims))])
    return loudness


def noise(rng, extent, spread, reach, cuts=(), held_as=jnp.bfloat16):
    values = jax.random.normal(rng, extent, jnp.float32) * spread
    if len(cuts) > 0:
        values = block_levels(rng, extent, cuts, -0.22, 0.18) * values
    return jnp.clip(values, min=-reach, max=reach).astype(held_as)


def setup_inputs(seed: int = 0, part: int = 0) -> dict:
    arg_keys = jax.random.split(jax.random.key(seed), 3)
    own_keys = jax.random.split(jax.random.fold_in(arg_keys[2], part), 3)
    return {
        "fields": noise(own_keys[0], (C, NX, NY * NZ), 1.0, 6.0, ((0, 4), (1, 4))),
        "conv_weight": noise(arg_keys[1], (27, C, C), (27 * C) ** -0.5, 0.0390625, ((1, 4), (2, 4))),
    }


def reference(fields, conv_weight):
    depth = fields.shape[1]
    source = fields.astype(jnp.float32).reshape(C, depth, NY, NZ)
    padded = jnp.pad(source, ((0, 0), (1, 1), (1, 1), (1, 1)))
    summed = jnp.zeros((C, depth * NY * NZ), jnp.float32)
    for step_x in range(3):
        for step_y in range(3):
            for step_z in range(3):
                matrix = conv_weight[9 * step_x + 3 * step_y + step_z].astype(jnp.float32)
                window = padded[:, step_x:step_x + depth, step_y:step_y + NY, step_z:step_z + NZ].reshape(C, depth * NY * NZ)
                summed = summed + jnp.dot(matrix, window, precision=lax.Precision.HIGHEST, preferred_element_type=jnp.float32)
    return summed.reshape(C, depth, NY * NZ).astype(jnp.bfloat16)
```

```python
import functools

import jax
import jax.numpy as jnp
from jax import lax
from jax.experimental import pallas as pl
from jax.experimental.pallas import tpu as pltpu
from jax.sharding import PartitionSpec as P

NY = 16
NZ = 16
CUTS = (0, 9, 16)
VMEM_LIMIT = 48 * 2**20


def bit_count(n):
    return n.bit_length() - 1


def reversed_bits(value, bits):
    out = 0
    for bit in range(bits):
        out = out | (((value >> bit) & 1) << (bits - 1 - bit))
    return out


def transpose_kernel(cuts, fields_ref, *out_refs):
    for plane in range(fields_ref.shape[1]):
        turned = fields_ref[:, plane, :].T
        for out_ref, low, high in zip(out_refs, cuts, cuts[1:]):
            out_ref[plane] = turned[low * NZ : high * NZ]


def by_cell(fields, cuts):
    count, depth, _ = fields.shape
    return pl.pallas_call(
        functools.partial(transpose_kernel, cuts),
        out_shape=[
            jax.ShapeDtypeStruct((depth, (high - low) * NZ, count), fields.dtype)
            for low, high in zip(cuts, cuts[1:])
        ],
        name="by_cell",
    )(fields)


def shifted(value, step):
    rows = value.shape[0]
    z = lax.broadcasted_iota(jnp.int32, value.shape, 0) % NZ
    inside = (z != NZ - 1) if step > 0 else (z != 0)
    rolled = pltpu.roll(value.astype(jnp.float32), (-step) % rows, 0)
    return jnp.where(inside, rolled, 0.0).astype(value.dtype)


def partial_kernel(plan, place_ref, *refs):
    ns, nc, cuts, index = plan
    repeats = nc // ns
    bits = bit_count(ns)
    low, high = cuts[index], cuts[index + 1]
    first = max(low - 1, 0)
    last = high if high == NY else high - 1
    top = first - 1
    part_refs = refs[: nc * (2 if index else 1)]
    weight_ref, mate_ref, keep_ref, window_ref = refs[len(part_refs) :]
    older_refs, newer_refs = part_refs[:-nc], part_refs[-nc:]
    depth = newer_refs[0].shape[0]
    count = newer_refs[0].shape[2]
    taken = repeats * count
    planes = ns * depth
    space, chan = place_ref[0], place_ref[1]
    zeros = jnp.zeros(window_ref.shape[1:], window_ref.dtype)
    window_ref[0] = zeros
    window_ref[planes + 1] = zeros
    edge = jnp.zeros((planes, NZ, window_ref.shape[2]), window_ref.dtype)
    if top < 0:
        window_ref[1 : planes + 1, 0:NZ, :] = edge
    if last == NY:
        window_ref[1 : planes + 1, (NY - top) * NZ : (NY - top + 1) * NZ, :] = edge

    def put(values, row, plane, turn):
        rows = values.shape[0]
        for step in range(3):
            piece = values if step == 1 else shifted(values, step - 1)
            for slot in range(repeats):
                begin = step * taken + slot * count

                def store():
                    window_ref[
                        plane, (row - top) * NZ : (row - top) * NZ + rows, begin : begin + count
                    ] = piece

                if repeats == 1:
                    store()
                else:
                    pl.when(turn == slot)(store)

    for round_index in range(nc):
        mask, jump = round_index % ns, round_index // ns
        source = reversed_bits((chan % ns) ^ mask, bits)
        turn = (jump + chan // ns) % repeats
        for plane in range(depth):
            where = 1 + source * depth + plane
            if index:
                begin = max(top, 0)
                older = older_refs[round_index]
                put(older[plane, (begin - cuts[index - 1]) * NZ :, :], begin, where, turn)
            put(newer_refs[round_index][plane], low, where, turn)

    half = ns // 2
    cells = (last - first) * NZ
    for position in range(ns):
        order = position % half
        owner = space ^ (2 * (half - 1 - order) + (1 if position < half else 0))
        total = None
        for pair in range(9):
            a, b = divmod(pair, 3)
            left = window_ref[
                pl.ds(depth * owner + a, depth), b * NZ : b * NZ + cells, :
            ].reshape(depth * cells, 3 * taken)
            right = jnp.concatenate([weight_ref[3 * pair + c] for c in range(3)], axis=1)
            product = lax.dot_general(
                left, right, (((1,), (1,)), ((), ())), preferred_element_type=jnp.float32
            )
            total = product if total is None else total + product
        target = mate_ref if position < half else keep_ref
        target[order * depth : (order + 1) * depth] = total.reshape(depth, cells, -1)


def partial_sums(place, older, newer, weights, plan):
    ns, nc, cuts, index = plan
    low, high = cuts[index], cuts[index + 1]
    first = max(low - 1, 0)
    last = high if high == NY else high - 1
    depth, _, count = newer[0].shape
    owned, taken = weights.shape[1:]
    cells = (last - first) * NZ
    in_vmem = pl.BlockSpec(memory_space=pltpu.VMEM)
    parts = [*older, *newer]
    flops = 2 * 27 * ns * depth * cells * owned * taken
    return pl.pallas_call(
        functools.partial(partial_kernel, plan),
        out_shape=[jax.ShapeDtypeStruct((ns // 2 * depth, cells, owned), jnp.float32)] * 2,
        in_specs=[pl.BlockSpec(memory_space=pltpu.SMEM)] + [in_vmem] * (len(parts) + 1),
        out_specs=[in_vmem] * 2,
        scratch_shapes=[
            pltpu.VMEM((ns * depth + 2, cells + 2 * NZ, 3 * taken), newer[0].dtype)
        ],
        compiler_params=pltpu.CompilerParams(vmem_limit_bytes=VMEM_LIMIT),
        cost_estimate=pl.CostEstimate(
            flops=flops, bytes_accessed=2 * weights.size, transcendentals=0
        ),
        name="partial_sums",
    )(place, *parts, weights)


def finish_kernel(counts, *refs):
    out_ref = refs[-1]
    for plane in range(out_ref.shape[1]):
        at = 0
        begin = 0
        for count in counts:
            pieces = refs[at : at + count]
            at += count
            total = pieces[0][plane]
            for piece in pieces[1:]:
                total = total + piece[plane]
            turned = total.T.astype(out_ref.dtype)
            out_ref[:, plane, begin : begin + turned.shape[1]] = turned
            begin += turned.shape[1]


def finish(groups, dtype):
    depth, _, owned = groups[0][0].shape
    cells = sum(pieces[0].shape[1] for pieces in groups)
    return pl.pallas_call(
        functools.partial(finish_kernel, [len(pieces) for pieces in groups]),
        out_shape=jax.ShapeDtypeStruct((owned, depth, cells), dtype),
        name="finish",
    )(*[piece for pieces in groups for piece in pieces])


def swapped(value, bit, ns):
    return lax.ppermute(value, "space", [(i, i ^ (1 << bit)) for i in range(ns)])


def local(fields, conv_weight):
    ns, nc = lax.axis_size("space"), lax.axis_size("chan")
    repeats = nc // ns
    bits = bit_count(ns)
    depth = fields.shape[1]
    place = jnp.stack([lax.axis_index("space"), lax.axis_index("chan")]).astype(jnp.int32)
    blocks = by_cell(fields, CUTS)
    received = []
    for index, block in enumerate(blocks):
        arrived = []
        for round_index in range(nc):
            mask, jump = round_index % ns, round_index // ns
            pairs = []
            for s in range(ns):
                for z in range(nc):
                    source = reversed_bits((z % ns) ^ mask, bits)
                    turn = (jump + z // ns) % repeats
                    pairs.append((source * nc + s * repeats + turn, s * nc + z))
            operand = block
            if index:
                operand, received[-1][round_index] = lax.optimization_barrier(
                    (block, received[-1][round_index])
                )
            arrived.append(lax.ppermute(operand, ("space", "chan"), pairs))
        received.append(arrived)
    groups = []
    for index, newer in enumerate(received):
        older = received[index - 1] if index else []
        mate, keep = partial_sums(place, older, newer, conv_weight, (ns, nc, CUTS, index))
        held = [keep]
        sent = [mate]
        for step, bit in enumerate([0, *range(bits - 1, 0, -1)]):
            arrived = [swapped(value, bit, ns) for value in sent]
            if step == bits - 1:
                held.extend(arrived)
                break
            total = sum(arrived, start=sum(held[1:], start=held[0]))
            middle = total.shape[0] // 2
            sent, held = [total[:middle]], [total[middle:]]
        groups.append(held)
    return finish(groups, fields.dtype)


def solution(mesh):
    return jax.shard_map(
        local,
        mesh=mesh,
        in_specs=(P("chan", ("groups", "space"), None), P(None, "chan", "space")),
        out_specs=P("chan", ("groups", "space"), None),
        check_vma=False,
    )
```

```python
import functools

import jax
import jax.numpy as jnp
from jax import lax
from jax.experimental import pallas as pl
from jax.experimental.pallas import tpu as pltpu
from jax.sharding import PartitionSpec as P

NY = 16
NZ = 16
CUTS = (0, 9, 16)
VMEM_LIMIT = 16 * 2**20
IN_VMEM = pl.BlockSpec(memory_space=pltpu.VMEM)


def bit_count(n):
    return n.bit_length() - 1


def reversed_bits(value, bits):
    out = 0
    for bit in range(bits):
        out = out | (((value >> bit) & 1) << (bits - 1 - bit))
    return out


def transpose_kernel(cuts, fields_ref, *out_refs):
    fields = fields_ref[...].astype(jnp.float32)
    for plane in range(fields_ref.shape[1]):
        turned = fields[:, plane, :].T.astype(fields_ref.dtype)
        for out_ref, low, high in zip(out_refs, cuts, cuts[1:]):
            out_ref[plane] = turned[low * NZ : high * NZ]


def by_cell(fields, cuts):
    count, depth, _ = fields.shape
    return pl.pallas_call(
        functools.partial(transpose_kernel, cuts),
        out_shape=[
            jax.ShapeDtypeStruct((depth, (high - low) * NZ, count), fields.dtype)
            for low, high in zip(cuts, cuts[1:])
        ],
        in_specs=[IN_VMEM],
        out_specs=[IN_VMEM] * (len(cuts) - 1),
        compiler_params=pltpu.CompilerParams(vmem_limit_bytes=VMEM_LIMIT // 2),
        name="by_cell",
    )(fields)


def hold_kernel(block_ref, weight_ref, token_ref):
    token_ref[...] = jnp.zeros(token_ref.shape, token_ref.dtype)


def hold(block, weights):
    return pl.pallas_call(
        hold_kernel,
        out_shape=jax.ShapeDtypeStruct((8, 128), jnp.float32),
        in_specs=[pl.BlockSpec(memory_space=pl.ANY), IN_VMEM],
        out_specs=IN_VMEM,
        compiler_params=pltpu.CompilerParams(vmem_limit_bytes=VMEM_LIMIT // 2),
        name="hold",
    )(block, weights)


def shifted(value, step):
    rows = value.shape[0]
    z = lax.broadcasted_iota(jnp.int32, value.shape, 0) % NZ
    inside = (z != NZ - 1) if step > 0 else (z != 0)
    rolled = pltpu.roll(value.astype(jnp.float32), (-step) % rows, 0)
    return jnp.where(inside, rolled, 0.0).astype(value.dtype)


def partial_kernel(plan, token_ref, *refs):
    ns, nc, cuts, index = plan
    repeats = nc // ns
    bits = bit_count(ns)
    low, high = cuts[index], cuts[index + 1]
    first = max(low - 1, 0)
    last = high if high == NY else high - 1
    top = first - 1
    part_refs = refs[: nc * (2 if index else 1)]
    weight_ref, mate_ref, keep_ref, window_ref = refs[len(part_refs) :]
    older_refs, newer_refs = part_refs[:-nc], part_refs[-nc:]
    depth = newer_refs[0].shape[0]
    count = newer_refs[0].shape[2]
    taken = repeats * count
    planes = ns * depth
    space, chan = lax.axis_index("space"), lax.axis_index("chan")
    zeros = jnp.zeros(window_ref.shape[1:], window_ref.dtype)
    window_ref[0] = zeros
    window_ref[planes + 1] = zeros
    edge = jnp.zeros((planes, NZ, window_ref.shape[2]), window_ref.dtype)
    if top < 0:
        window_ref[1 : planes + 1, 0:NZ, :] = edge
    if last == NY:
        window_ref[1 : planes + 1, (NY - top) * NZ : (NY - top + 1) * NZ, :] = edge

    def put(values, row, plane, turn):
        rows = values.shape[0]
        for step in range(3):
            piece = values if step == 1 else shifted(values, step - 1)
            for slot in range(repeats):
                begin = step * taken + slot * count

                def store():
                    window_ref[
                        plane, (row - top) * NZ : (row - top) * NZ + rows, begin : begin + count
                    ] = piece

                if repeats == 1:
                    store()
                else:
                    pl.when(turn == slot)(store)

    for round_index in range(nc):
        mask, jump = round_index % ns, round_index // ns
        source = reversed_bits((chan % ns) ^ mask, bits)
        turn = (jump + chan // ns) % repeats
        for plane in range(depth):
            where = 1 + source * depth + plane
            if index:
                begin = max(top, 0)
                older = older_refs[round_index]
                put(older[plane, (begin - cuts[index - 1]) * NZ :, :], begin, where, turn)
            put(newer_refs[round_index][plane], low, where, turn)

    half = ns // 2
    cells = (last - first) * NZ
    for order in range(half):
        owners = [space ^ (2 * (half - 1 - order) + core) for core in (1, 0)]
        total = None
        for pair in range(9):
            a, b = divmod(pair, 3)
            left = jnp.concatenate(
                [
                    window_ref[
                        pl.ds(depth * owner + a, depth), b * NZ : b * NZ + cells, :
                    ].reshape(depth * cells, 3 * taken)
                    for owner in owners
                ],
                axis=0,
            )
            right = jnp.concatenate([weight_ref[3 * pair + c] for c in range(3)], axis=1)
            product = lax.dot_general(
                left, right, (((1,), (1,)), ((), ())), preferred_element_type=jnp.float32
            )
            total = product if total is None else total + product
        total = total.reshape(2, depth, cells, -1)
        mate_ref[order * depth : (order + 1) * depth] = total[0]
        keep_ref[order * depth : (order + 1) * depth] = total[1]


def partial_sums(token, older, newer, weights, plan):
    ns, nc, cuts, index = plan
    low, high = cuts[index], cuts[index + 1]
    first = max(low - 1, 0)
    last = high if high == NY else high - 1
    depth, _, count = newer[0].shape
    owned, taken = weights.shape[1:]
    cells = (last - first) * NZ
    in_vmem = pl.BlockSpec(memory_space=pltpu.VMEM)
    parts = [*older, *newer]
    flops = 2 * 27 * ns * depth * cells * owned * taken
    return pl.pallas_call(
        functools.partial(partial_kernel, plan),
        out_shape=[jax.ShapeDtypeStruct((ns // 2 * depth, cells, owned), jnp.float32)] * 2,
        in_specs=[pl.BlockSpec(memory_space=pl.ANY)] + [in_vmem] * (len(parts) + 1),
        out_specs=[in_vmem] * 2,
        scratch_shapes=[
            pltpu.VMEM((ns * depth + 2, cells + 2 * NZ, 3 * taken), newer[0].dtype)
        ],
        compiler_params=pltpu.CompilerParams(vmem_limit_bytes=VMEM_LIMIT),
        cost_estimate=pl.CostEstimate(
            flops=flops, bytes_accessed=2 * weights.size, transcendentals=0
        ),
        name="partial_sums",
    )(token, *parts, weights)


def finish_kernel(counts, *refs):
    *refs, out_ref, turned_ref = refs
    for plane in range(out_ref.shape[1]):
        at = 0
        begin = 0
        for count in counts:
            pieces = refs[at : at + count]
            at += count
            total = pieces[0][plane]
            for piece in pieces[1:]:
                total = total + piece[plane]
            turned_ref[:, plane, begin : begin + total.shape[0]] = total.T
            begin += total.shape[0]
    out_ref[...] = turned_ref[...].astype(out_ref.dtype)


def finish(groups, dtype):
    depth, _, owned = groups[0][0].shape
    cells = sum(pieces[0].shape[1] for pieces in groups)
    flat = [piece for pieces in groups for piece in pieces]
    return pl.pallas_call(
        functools.partial(finish_kernel, [len(pieces) for pieces in groups]),
        out_shape=jax.ShapeDtypeStruct((owned, depth, cells), dtype),
        in_specs=[IN_VMEM] * len(flat),
        out_specs=IN_VMEM,
        scratch_shapes=[pltpu.VMEM((owned, depth, cells), jnp.float32)],
        compiler_params=pltpu.CompilerParams(vmem_limit_bytes=VMEM_LIMIT // 2),
        name="finish",
    )(*flat)


def swapped(value, bit, ns):
    return lax.ppermute(value, "space", [(i, i ^ (1 << bit)) for i in range(ns)])


def local(fields, conv_weight):
    ns, nc = lax.axis_size("space"), lax.axis_size("chan")
    repeats = nc // ns
    bits = bit_count(ns)
    depth = fields.shape[1]
    blocks = by_cell(fields, CUTS)
    token = hold(blocks[0], conv_weight)
    received = []
    for index, block in enumerate(blocks):
        arrived = []
        for round_index in range(nc):
            mask, jump = round_index % ns, round_index // ns
            pairs = []
            for s in range(ns):
                for z in range(nc):
                    source = reversed_bits((z % ns) ^ mask, bits)
                    turn = (jump + z // ns) % repeats
                    pairs.append((source * nc + s * repeats + turn, s * nc + z))
            arrived.append(lax.ppermute(block, ("space", "chan"), pairs))
        received.append(arrived)
    groups = []
    for index, newer in enumerate(received):
        older = received[index - 1] if index else []
        mate, keep = partial_sums(token, older, newer, conv_weight, (ns, nc, CUTS, index))
        token, mate = lax.optimization_barrier((token, mate))
        held = [keep]
        sent = [mate]
        for step, bit in enumerate([0, *range(bits - 1, 0, -1)]):
            arrived = [swapped(value, bit, ns) for value in sent]
            if step == bits - 1:
                held.extend(arrived)
                break
            total = sum(arrived, start=sum(held[1:], start=held[0]))
            middle = total.shape[0] // 2
            sent, held = [total[:middle]], [total[middle:]]
        groups.append(held)
    return finish(groups, fields.dtype)


def solution(mesh):
    return jax.shard_map(
        local,
        mesh=mesh,
        in_specs=(P("chan", ("groups", "space"), None), P(None, "chan", "space")),
        out_specs=P("chan", ("groups", "space"), None),
        check_vma=False,
    )
```

```python
import functools

import jax
import jax.numpy as jnp
from jax import lax
from jax.experimental import pallas as pl
from jax.experimental.pallas import tpu as pltpu
from jax.sharding import PartitionSpec as P

NY = 16
NZ = 16
CUTS = (0, 9, 16)
HEAD = 16
LOWEST, SPAN = 14.0, 29.0
VMEM_LIMIT = 16 * 2**20
IN_VMEM = pl.BlockSpec(memory_space=pltpu.VMEM)


def bit_count(n):
    return n.bit_length() - 1


def reversed_bits(value, bits):
    out = 0
    for bit in range(bits):
        out = out | (((value >> bit) & 1) << (bits - 1 - bit))
    return out


def transpose_kernel(cuts, fields_ref, *out_refs):
    fields = fields_ref[...].astype(jnp.float32)
    for plane in range(fields_ref.shape[1]):
        turned = fields[:, plane, :].T.astype(fields_ref.dtype)
        for out_ref, low, high in zip(out_refs, cuts, cuts[1:]):
            out_ref[plane] = turned[low * NZ : high * NZ]


def by_cell(fields, cuts):
    count, depth, _ = fields.shape
    return pl.pallas_call(
        functools.partial(transpose_kernel, cuts),
        out_shape=[
            jax.ShapeDtypeStruct((depth, (high - low) * NZ, count), fields.dtype)
            for low, high in zip(cuts, cuts[1:])
        ],
        in_specs=[IN_VMEM],
        out_specs=[IN_VMEM] * (len(cuts) - 1),
        compiler_params=pltpu.CompilerParams(vmem_limit_bytes=VMEM_LIMIT // 2),
        name="by_cell",
    )(fields)


def hold_kernel(block_ref, weight_ref, token_ref):
    token_ref[...] = jnp.zeros(token_ref.shape, token_ref.dtype)


def hold(block, weights):
    return pl.pallas_call(
        hold_kernel,
        out_shape=jax.ShapeDtypeStruct((8, 128), jnp.float32),
        in_specs=[pl.BlockSpec(memory_space=pl.ANY), IN_VMEM],
        out_specs=IN_VMEM,
        compiler_params=pltpu.CompilerParams(vmem_limit_bytes=VMEM_LIMIT // 2),
        name="hold",
    )(block, weights)


def shifted(value, step):
    rows = value.shape[0]
    z = lax.broadcasted_iota(jnp.int32, value.shape, 0) % NZ
    inside = (z != NZ - 1) if step > 0 else (z != 0)
    rolled = pltpu.roll(value.astype(jnp.float32), (-step) % rows, 0)
    return jnp.where(inside, rolled, 0.0).astype(value.dtype)


def fill_window(plan, part_refs, window_ref):
    ns, nc, cuts, index = plan
    repeats = nc // ns
    bits = bit_count(ns)
    low, high = cuts[index], cuts[index + 1]
    first = max(low - 1, 0)
    last = high if high == NY else high - 1
    top = first - 1
    older_refs, newer_refs = part_refs[:-nc], part_refs[-nc:]
    depth = newer_refs[0].shape[0]
    count = newer_refs[0].shape[2]
    taken = repeats * count
    planes = ns * depth
    chan = lax.axis_index("chan")
    zeros = jnp.zeros(window_ref.shape[1:], window_ref.dtype)
    window_ref[0] = zeros
    window_ref[planes + 1] = zeros
    edge = jnp.zeros((planes, NZ, window_ref.shape[2]), window_ref.dtype)
    if top < 0:
        window_ref[1 : planes + 1, 0:NZ, :] = edge
    if last == NY:
        window_ref[1 : planes + 1, (NY - top) * NZ : (NY - top + 1) * NZ, :] = edge

    def put(values, row, plane, turn):
        rows = values.shape[0]
        for step in range(3):
            piece = values if step == 1 else shifted(values, step - 1)
            for slot in range(repeats):
                begin = step * taken + slot * count

                def store():
                    window_ref[
                        plane, (row - top) * NZ : (row - top) * NZ + rows, begin : begin + count
                    ] = piece

                if repeats == 1:
                    store()
                else:
                    pl.when(turn == slot)(store)

    for round_index in range(nc):
        mask, jump = round_index % ns, round_index // ns
        source = reversed_bits((chan % ns) ^ mask, bits)
        turn = (jump + chan // ns) % repeats
        for plane in range(depth):
            where = 1 + source * depth + plane
            if index:
                begin = max(top, 0)
                older = older_refs[round_index]
                put(older[plane, (begin - cuts[index - 1]) * NZ :, :], begin, where, turn)
            put(newer_refs[round_index][plane], low, where, turn)

def add_up(plan, far, weight_ref, window_ref, mate_ref, keep_ref):
    ns, nc, cuts, index = plan
    depth = (window_ref.shape[0] - 2) // ns
    cells = window_ref.shape[1] - 2 * NZ
    space = lax.axis_index("space")
    groups = ns // 4
    for order in range(groups):
        mask = 2 * (groups - 1 - order + (groups if far else 0))
        owners = [space ^ (mask + 1), space ^ mask]
        total = None
        for pair in range(9):
            a, b = divmod(pair, 3)
            left = jnp.concatenate(
                [
                    window_ref[
                        pl.ds(depth * owner + a, depth), b * NZ : b * NZ + cells, :
                    ].reshape(depth * cells, -1)
                    for owner in owners
                ],
                axis=0,
            )
            right = jnp.concatenate([weight_ref[3 * pair + c] for c in range(3)], axis=1)
            product = lax.dot_general(
                left, right, (((1,), (1,)), ((), ())), preferred_element_type=jnp.float32
            )
            total = product if total is None else total + product
        begin, rows = HEAD + order * depth * cells, depth * cells
        mate_ref[begin : begin + rows] = total[:rows]
        keep_ref[begin : begin + rows] = total[rows:]
    for ref in (mate_ref, keep_ref):
        peak = jnp.max(jnp.abs(ref[HEAD:]), axis=0, keepdims=True)
        ref[:HEAD] = jnp.broadcast_to(peak, (HEAD, ref.shape[1]))


def first_kernel(plan, token_ref, weight_ref, *refs):
    *part_refs, mate_ref, keep_ref, window_ref = refs
    fill_window(plan, part_refs, window_ref)
    add_up(plan, True, weight_ref, window_ref, mate_ref, keep_ref)


def second_kernel(plan, token_ref, weight_ref, window_ref, mate_ref, keep_ref):
    add_up(plan, False, weight_ref, window_ref, mate_ref, keep_ref)


def both_kernel(plan, token_ref, weight_ref, *refs):
    *part_refs, far_mate, far_keep, near_mate, near_keep, window_ref = refs
    fill_window(plan, part_refs, window_ref)
    add_up(plan, True, weight_ref, window_ref, far_mate, far_keep)
    add_up(plan, False, weight_ref, window_ref, near_mate, near_keep)


def partial_sums(token, older, newer, weights, plan, at_once):
    ns, nc, cuts, index = plan
    low, high = cuts[index], cuts[index + 1]
    first = max(low - 1, 0)
    last = high if high == NY else high - 1
    depth = newer[0].shape[0]
    owned, taken = weights.shape[1:]
    cells = (last - first) * NZ
    sums = jax.ShapeDtypeStruct((HEAD + ns // 4 * depth * cells, owned), jnp.float32)
    window = (ns * depth + 2, cells + 2 * NZ, 3 * taken)

    def call(kernel, inputs, out_shape, scratch_shapes):
        return pl.pallas_call(
            functools.partial(kernel, plan),
            out_shape=out_shape,
            in_specs=[pl.BlockSpec(memory_space=pl.ANY)] + [IN_VMEM] * (1 + len(inputs)),
            out_specs=[IN_VMEM] * len(out_shape),
            scratch_shapes=scratch_shapes,
            compiler_params=pltpu.CompilerParams(vmem_limit_bytes=VMEM_LIMIT),
            cost_estimate=pl.CostEstimate(
                flops=27 * len(out_shape) // 2 * ns * depth * cells * owned * taken,
                bytes_accessed=2 * weights.size,
                transcendentals=0,
            ),
            name="partial_sums",
        )(token, weights, *inputs)

    parts = [*older, *newer]
    if at_once:
        far_mate, far_keep, near_mate, near_keep = call(
            both_kernel, parts, [sums] * 4, [pltpu.VMEM(window, weights.dtype)]
        )
    else:
        far_mate, far_keep, filled = call(
            first_kernel, parts, [sums] * 2 + [jax.ShapeDtypeStruct(window, weights.dtype)], []
        )
        near_mate, near_keep = call(second_kernel, [filled], [sums] * 2, [])
    return (far_mate, far_keep), (near_mate, near_keep)


def finish_kernel(counts, *refs):
    *refs, out_ref, turned_ref = refs
    at = begin = 0
    for count in counts:
        pieces = refs[at : at + count]
        at += count
        cells = pieces[0].shape[0] // out_ref.shape[1]
        for plane in range(out_ref.shape[1]):
            total = pieces[0][plane * cells : (plane + 1) * cells]
            for piece in pieces[1:]:
                total = total + piece[plane * cells : (plane + 1) * cells]
            turned_ref[:, plane, begin : begin + cells] = total.T
        begin += cells
    out_ref[...] = turned_ref[...].astype(out_ref.dtype)


def finish(groups, depth, dtype):
    owned = groups[0][0].shape[1]
    cells = sum(pieces[0].shape[0] for pieces in groups) // depth
    flat = [piece for pieces in groups for piece in pieces]
    return pl.pallas_call(
        functools.partial(finish_kernel, [len(pieces) for pieces in groups]),
        out_shape=jax.ShapeDtypeStruct((owned, depth, cells), dtype),
        in_specs=[IN_VMEM] * len(flat),
        out_specs=IN_VMEM,
        scratch_shapes=[pltpu.VMEM((owned, depth, cells), jnp.float32)],
        compiler_params=pltpu.CompilerParams(vmem_limit_bytes=VMEM_LIMIT // 2),
        name="finish",
    )(*flat)


def level(head):
    exponent, fraction = head[:1].astype(jnp.float32), head[HEAD // 2 : HEAD // 2 + 1]
    return fraction.astype(jnp.float32) * jnp.exp2(exponent)


def coded(sums):
    bound = jnp.maximum(sums[:HEAD], 1e-30)
    exponent = jnp.floor(jnp.log2(bound))
    fraction = bound * jnp.exp2(-exponent) * (1 + 2.0**-10)
    row = lax.broadcasted_iota(jnp.int32, bound.shape, 0)
    head = jnp.where(row < HEAD // 2, exponent, fraction).astype(jnp.float16)
    values = sums[HEAD:]
    power = jnp.exp2(jnp.minimum(jnp.abs(values) / level(head), 1.0) * SPAN - LOWEST)
    return jnp.concatenate([head, jnp.where(values < 0, -power, power).astype(jnp.float16)])


def decoded(sent):
    values = sent[HEAD:].astype(jnp.float32)
    size = (jnp.log2(jnp.abs(values)) + LOWEST) * (level(sent[:HEAD]) / SPAN)
    return jnp.where(values < 0, -size, size)


def swapped(value, bit, ns):
    return lax.ppermute(value, "space", [(i, i ^ (1 << bit)) for i in range(ns)])


def local(fields, conv_weight):
    ns, nc = lax.axis_size("space"), lax.axis_size("chan")
    repeats = nc // ns
    bits = bit_count(ns)
    depth = fields.shape[1]
    blocks = by_cell(fields, CUTS)
    token = hold(blocks[0], conv_weight)
    received = []
    for index, block in enumerate(blocks):
        arrived = []
        for round_index in range(nc):
            mask, jump = round_index % ns, round_index // ns
            pairs = []
            for s in range(ns):
                for z in range(nc):
                    source = reversed_bits((z % ns) ^ mask, bits)
                    turn = (jump + z // ns) % repeats
                    pairs.append((source * nc + s * repeats + turn, s * nc + z))
            arrived.append(lax.ppermute(block, ("space", "chan"), pairs))
        received.append(arrived)
    groups = []
    for index, newer in enumerate(received):
        older = received[index - 1] if index else []
        plan = (ns, nc, CUTS, index)
        far, near = partial_sums(token, older, newer, conv_weight, plan, index == 0)
        token, mate = lax.optimization_barrier((token, far[0]))
        far = (mate, far[1])
        far, near = [keep + swapped(mate, 0, ns) for mate, keep in (far, near)]
        for bit in range(bits - 1, 1, -1):
            total = near + swapped(far, bit, ns)
            middle = HEAD + (total.shape[0] - HEAD) // 2
            far, near = total[:middle], jnp.concatenate([total[:HEAD], total[middle:]])
        groups.append([near[HEAD:], decoded(swapped(coded(far), 1, ns))])
    return finish(groups, fields.shape[1], fields.dtype)


def solution(mesh):
    return jax.shard_map(
        local,
        mesh=mesh,
        in_specs=(P("chan", ("groups", "space"), None), P(None, "chan", "space")),
        out_specs=P("chan", ("groups", "space"), None),
        check_vma=False,
    )
```

```python
import functools

import jax
import jax.numpy as jnp
from jax import lax
from jax.experimental import pallas as pl
from jax.experimental.pallas import tpu as pltpu
from jax.sharding import PartitionSpec as P

NY = 16
NZ = 16
CUTS = (0, 9, 16)
STEPS = [[(True, (1, 0))], [(False, (1,))], [(False, (0,))]]
HEAD = 16
LOWEST, SPAN = 14.0, 29.0
VMEM_LIMIT = 16 * 2**20
IN_VMEM = pl.BlockSpec(memory_space=pltpu.VMEM)


def bit_count(n):
    return n.bit_length() - 1


def reversed_bits(value, bits):
    out = 0
    for bit in range(bits):
        out = out | (((value >> bit) & 1) << (bits - 1 - bit))
    return out


def paired(index):
    return index > 0


def rounds_of(index, nc):
    return nc // 2 if paired(index) else nc


def sender(index, chan, round_index, ns, nc):
    masks = ns // 2 if paired(index) else ns
    mask, jump = round_index % masks, round_index // masks
    source = reversed_bits(chan % ns, bit_count(ns)) ^ (2 * mask if paired(index) else mask)
    return source, (jump + chan // ns) % (nc // ns)


def pair_kernel(own_ref, mate_ref, out_ref):
    depth = own_ref.shape[0]
    core = lax.axis_index("space") % 2
    out_ref[pl.ds(depth * core, depth)] = own_ref[...]
    out_ref[pl.ds(depth * (1 - core), depth)] = mate_ref[...]


def pair(own, mate):
    depth, cells, count = own.shape
    return pl.pallas_call(
        pair_kernel,
        out_shape=jax.ShapeDtypeStruct((2 * depth, cells, count), own.dtype),
        in_specs=[IN_VMEM] * 2,
        out_specs=IN_VMEM,
        compiler_params=pltpu.CompilerParams(vmem_limit_bytes=VMEM_LIMIT // 2),
        name="pair",
    )(own, mate)


def sent_parts(block, index, ns, nc):
    payload = pair(block, swapped(block, 0, ns)) if paired(index) else block
    parts = []
    for round_index in range(rounds_of(index, nc)):
        pairs = []
        for s in range(ns):
            for z in range(nc):
                source, turn = sender(index, z, round_index, ns, nc)
                pairs.append((source * nc + s * (nc // ns) + turn, s * nc + z))
        parts.append(lax.ppermute(payload, ("space", "chan"), pairs))
    return parts


def transpose_kernel(cuts, fields_ref, *out_refs):
    fields = fields_ref[...].astype(jnp.float32)
    for plane in range(fields_ref.shape[1]):
        turned = fields[:, plane, :].T.astype(fields_ref.dtype)
        for out_ref, low, high in zip(out_refs, cuts, cuts[1:]):
            out_ref[plane] = turned[low * NZ : high * NZ]


def by_cell(fields, cuts):
    count, depth, _ = fields.shape
    return pl.pallas_call(
        functools.partial(transpose_kernel, cuts),
        out_shape=[
            jax.ShapeDtypeStruct((depth, (high - low) * NZ, count), fields.dtype)
            for low, high in zip(cuts, cuts[1:])
        ],
        in_specs=[IN_VMEM],
        out_specs=[IN_VMEM] * (len(cuts) - 1),
        compiler_params=pltpu.CompilerParams(vmem_limit_bytes=VMEM_LIMIT // 2),
        name="by_cell",
    )(fields)


def hold_kernel(block_ref, weight_ref, token_ref):
    token_ref[...] = jnp.zeros(token_ref.shape, token_ref.dtype)


def hold(block, weights):
    return pl.pallas_call(
        hold_kernel,
        out_shape=jax.ShapeDtypeStruct((8, 128), jnp.float32),
        in_specs=[pl.BlockSpec(memory_space=pl.ANY), IN_VMEM],
        out_specs=IN_VMEM,
        compiler_params=pltpu.CompilerParams(vmem_limit_bytes=VMEM_LIMIT // 2),
        name="hold",
    )(block, weights)


def shifted(value, step):
    rows = value.shape[0]
    z = lax.broadcasted_iota(jnp.int32, value.shape, 0) % NZ
    inside = (z != NZ - 1) if step > 0 else (z != 0)
    rolled = pltpu.roll(value.astype(jnp.float32), (-step) % rows, 0)
    return jnp.where(inside, rolled, 0.0).astype(value.dtype)


def fill_window(plan, part_refs, window_ref):
    ns, nc, cuts, index = plan
    repeats = nc // ns
    low, high = cuts[index], cuts[index + 1]
    first = max(low - 1, 0)
    last = high if high == NY else high - 1
    top = first - 1
    depth = (window_ref.shape[0] - 2) // ns
    count = part_refs[0].shape[2]
    taken = repeats * count
    planes = ns * depth
    chan = lax.axis_index("chan")
    zeros = jnp.zeros(window_ref.shape[1:], window_ref.dtype)
    window_ref[0] = zeros
    window_ref[planes + 1] = zeros
    edge = jnp.zeros((planes, NZ, window_ref.shape[2]), window_ref.dtype)
    if top < 0:
        window_ref[1 : planes + 1, 0:NZ, :] = edge
    if last == NY:
        window_ref[1 : planes + 1, (NY - top) * NZ : (NY - top + 1) * NZ, :] = edge

    def put(values, row, plane, turn):
        rows = values.shape[0]
        for step in range(3):
            piece = values if step == 1 else shifted(values, step - 1)
            for slot in range(repeats):
                begin = step * taken + slot * count

                def store():
                    window_ref[
                        plane, (row - top) * NZ : (row - top) * NZ + rows, begin : begin + count
                    ] = piece

                if repeats == 1:
                    store()
                else:
                    pl.when(turn == slot)(store)

    count_new = rounds_of(index, nc)
    sets = [(index, part_refs[-count_new:])]
    if index:
        sets.append((index - 1, part_refs[:-count_new]))
    for index_of, refs in sets:
        skipped = max(top - cuts[index_of], 0)
        for round_index, part_ref in enumerate(refs):
            source, turn = sender(index_of, chan, round_index, ns, nc)
            begin = (source // 2 * 2 if paired(index_of) else source) * depth
            for plane in range(part_ref.shape[0]):
                put(
                    part_ref[plane, skipped * NZ :, :],
                    cuts[index_of] + skipped,
                    1 + begin + plane,
                    turn,
                )


def add_up(plan, far, cores, weight_ref, window_ref, out_refs):
    ns, nc, cuts, index = plan
    depth = (window_ref.shape[0] - 2) // ns
    cells = window_ref.shape[1] - 2 * NZ
    space = lax.axis_index("space")
    groups = ns // 4
    for order in range(groups):
        mask = 2 * (groups - 1 - order + (groups if far else 0))
        total = None
        for pair in range(9):
            a, b = divmod(pair, 3)
            left = jnp.concatenate(
                [
                    window_ref[
                        pl.ds(depth * (space ^ (mask + core)) + a, depth),
                        b * NZ : b * NZ + cells,
                        :,
                    ].reshape(depth * cells, -1)
                    for core in cores
                ],
                axis=0,
            )
            right = jnp.concatenate([weight_ref[3 * pair + c] for c in range(3)], axis=1)
            product = lax.dot_general(
                left, right, (((1,), (1,)), ((), ())), preferred_element_type=jnp.float32
            )
            total = product if total is None else total + product
        begin, rows = HEAD + order * depth * cells, depth * cells
        for at, ref in enumerate(out_refs):
            ref[begin : begin + rows] = total[at * rows : (at + 1) * rows]
    for ref in out_refs:
        peak = jnp.max(jnp.abs(ref[HEAD:]), axis=0, keepdims=True)
        ref[:HEAD] = jnp.broadcast_to(peak, (HEAD, ref.shape[1]))


def first_kernel(plan, jobs, token_ref, weight_ref, *refs):
    *refs, window_ref = refs
    count = sum(len(cores) for _, cores in jobs)
    part_refs, out_refs = refs[:-count], refs[-count:]
    fill_window(plan, part_refs, window_ref)
    for far, cores in jobs:
        add_up(plan, far, cores, weight_ref, window_ref, out_refs[: len(cores)])
        out_refs = out_refs[len(cores) :]


def later_kernel(plan, jobs, token_ref, weight_ref, window_ref, *out_refs):
    for far, cores in jobs:
        add_up(plan, far, cores, weight_ref, window_ref, out_refs)


def partial_sums(token, older, newer, weights, depth, plan, at_once):
    ns, nc, cuts, index = plan
    low, high = cuts[index], cuts[index + 1]
    first = max(low - 1, 0)
    last = high if high == NY else high - 1
    owned, taken = weights.shape[1:]
    cells = (last - first) * NZ
    sums = jax.ShapeDtypeStruct((HEAD + ns // 4 * depth * cells, owned), jnp.float32)
    window = (ns * depth + 2, cells + 2 * NZ, 3 * taken)

    def call(kernel, jobs, inputs, out_shape, scratch_shapes, token=token):
        return pl.pallas_call(
            functools.partial(kernel, plan, jobs),
            out_shape=out_shape,
            in_specs=[pl.BlockSpec(memory_space=pl.ANY)] + [IN_VMEM] * (1 + len(inputs)),
            out_specs=[IN_VMEM] * len(out_shape),
            scratch_shapes=scratch_shapes,
            compiler_params=pltpu.CompilerParams(vmem_limit_bytes=VMEM_LIMIT),
            cost_estimate=pl.CostEstimate(
                flops=27 * 2 * sum(len(cores) for _, cores in jobs) * ns // 4 * depth * cells * owned * taken,
                bytes_accessed=2 * weights.size,
                transcendentals=0,
            ),
            name="partial_sums",
        )(token, weights, *inputs)

    parts = [*older, *newer]
    if at_once:
        jobs = [(True, (1, 0)), (False, (1, 0))]
        far_mate, far_keep, near_mate, near_keep = call(
            first_kernel, jobs, parts, [sums] * 4, [pltpu.VMEM(window, weights.dtype)]
        )
        return far_mate, far_keep, near_mate, lambda token: near_keep
    results = []
    for jobs in STEPS[:-1]:
        count = sum(len(cores) for _, cores in jobs)
        if not results:
            filled = jax.ShapeDtypeStruct(window, weights.dtype)
            *results, filled = call(first_kernel, jobs, parts, [sums] * count + [filled], [])
        else:
            results += call(later_kernel, jobs, [filled], [sums] * count, [])

    def last(token):
        return call(later_kernel, STEPS[-1], [filled], [sums], [], token)[0]

    return *results, last


def finish_kernel(counts, *refs):
    *refs, out_ref, turned_ref = refs
    at = begin = 0
    for count in counts:
        pieces = refs[at : at + count]
        at += count
        cells = pieces[0].shape[0] // out_ref.shape[1]
        for plane in range(out_ref.shape[1]):
            total = pieces[0][plane * cells : (plane + 1) * cells]
            for piece in pieces[1:]:
                total = total + piece[plane * cells : (plane + 1) * cells]
            turned_ref[:, plane, begin : begin + cells] = total.T
        begin += cells
    out_ref[...] = turned_ref[...].astype(out_ref.dtype)


def finish(groups, depth, dtype):
    owned = groups[0][0].shape[1]
    cells = sum(pieces[0].shape[0] for pieces in groups) // depth
    flat = [piece for pieces in groups for piece in pieces]
    return pl.pallas_call(
        functools.partial(finish_kernel, [len(pieces) for pieces in groups]),
        out_shape=jax.ShapeDtypeStruct((owned, depth, cells), dtype),
        in_specs=[IN_VMEM] * len(flat),
        out_specs=IN_VMEM,
        scratch_shapes=[pltpu.VMEM((owned, depth, cells), jnp.float32)],
        compiler_params=pltpu.CompilerParams(vmem_limit_bytes=VMEM_LIMIT // 2),
        name="finish",
    )(*flat)


def level(head):
    exponent, fraction = head[:1].astype(jnp.float32), head[HEAD // 2 : HEAD // 2 + 1]
    return fraction.astype(jnp.float32) * jnp.exp2(exponent)


def coded(sums):
    bound = jnp.maximum(sums[:HEAD], 1e-30)
    exponent = jnp.floor(jnp.log2(bound))
    fraction = bound * jnp.exp2(-exponent) * (1 + 2.0**-10)
    row = lax.broadcasted_iota(jnp.int32, bound.shape, 0)
    head = jnp.where(row < HEAD // 2, exponent, fraction).astype(jnp.float16)
    values = sums[HEAD:]
    power = jnp.exp2(jnp.minimum(jnp.abs(values) / level(head), 1.0) * SPAN - LOWEST)
    return jnp.concatenate([head, jnp.where(values < 0, -power, power).astype(jnp.float16)])


def decoded(sent):
    values = sent[HEAD:].astype(jnp.float32)
    size = (jnp.log2(jnp.abs(values)) + LOWEST) * (level(sent[:HEAD]) / SPAN)
    return jnp.where(values < 0, -size, size)


def swapped(value, bit, ns):
    return lax.ppermute(value, "space", [(i, i ^ (1 << bit)) for i in range(ns)])


def local(fields, conv_weight):
    ns, nc = lax.axis_size("space"), lax.axis_size("chan")
    repeats = nc // ns
    bits = bit_count(ns)
    depth = fields.shape[1]
    blocks = by_cell(fields, CUTS)
    token = hold(blocks[0], conv_weight)
    received = [sent_parts(block, index, ns, nc) for index, block in enumerate(blocks)]
    groups = []
    for index, newer in enumerate(received):
        older = received[index - 1] if index else []
        plan = (ns, nc, CUTS, index)
        far_mate, far_keep, near_mate, last = partial_sums(
            token, older, newer, conv_weight, depth, plan, index == 0
        )
        token, far_mate = lax.optimization_barrier((token, far_mate))
        far, after = far_keep + swapped(far_mate, 0, ns), token
        if bits == 2:
            sent = coded(far)
            after, sent = lax.optimization_barrier((token, sent))
        near = last(after) + swapped(near_mate, 0, ns)
        for bit in range(bits - 1, 1, -1):
            total = near + swapped(far, bit, ns)
            middle = HEAD + (total.shape[0] - HEAD) // 2
            far, near = total[:middle], jnp.concatenate([total[:HEAD], total[middle:]])
        if bits > 2:
            sent = coded(far)
        groups.append([near[HEAD:], decoded(swapped(sent, 1, ns))])
    return finish(groups, fields.shape[1], fields.dtype)


def solution(mesh):
    return jax.shard_map(
        local,
        mesh=mesh,
        in_specs=(P("chan", ("groups", "space"), None), P(None, "chan", "space")),
        out_specs=P("chan", ("groups", "space"), None),
        check_vma=False,
    )
```

```python
import functools

import jax
import jax.numpy as jnp
from jax import lax
from jax.experimental import pallas as pl
from jax.experimental.pallas import tpu as pltpu
from jax.sharding import PartitionSpec as P

NY = 16
NZ = 16
CUTS = (0, 9, 16)
STEPS = [[(True, (1,))], [(True, (0,)), (False, (1,))], [(False, (0,))]]
HEAD = 16
LOWEST, SPAN = 14.0, 29.0
VMEM_LIMIT = 16 * 2**20
IN_VMEM = pl.BlockSpec(memory_space=pltpu.VMEM)


def bit_count(n):
    return n.bit_length() - 1


def reversed_bits(value, bits):
    out = 0
    for bit in range(bits):
        out = out | (((value >> bit) & 1) << (bits - 1 - bit))
    return out


def paired(index):
    return index > 0


def rounds_of(index, nc):
    return nc // 2 if paired(index) else nc


def sender(index, chan, round_index, ns, nc):
    masks = ns // 2 if paired(index) else ns
    mask, jump = round_index % masks, round_index // masks
    source = reversed_bits(chan % ns, bit_count(ns)) ^ (2 * mask if paired(index) else mask)
    return source, (jump + chan // ns) % (nc // ns)


def pair_kernel(own_ref, mate_ref, out_ref):
    depth = own_ref.shape[0]
    core = lax.axis_index("space") % 2
    out_ref[pl.ds(depth * core, depth)] = own_ref[...]
    out_ref[pl.ds(depth * (1 - core), depth)] = mate_ref[...]


def pair(own, mate):
    depth, cells, count = own.shape
    return pl.pallas_call(
        pair_kernel,
        out_shape=jax.ShapeDtypeStruct((2 * depth, cells, count), own.dtype),
        in_specs=[IN_VMEM] * 2,
        out_specs=IN_VMEM,
        compiler_params=pltpu.CompilerParams(vmem_limit_bytes=VMEM_LIMIT // 2),
        name="pair",
    )(own, mate)


def sent_parts(block, index, ns, nc):
    payload = pair(block, swapped(block, 0, ns)) if paired(index) else block
    parts = []
    for round_index in range(rounds_of(index, nc)):
        pairs = []
        for s in range(ns):
            for z in range(nc):
                source, turn = sender(index, z, round_index, ns, nc)
                pairs.append((source * nc + s * (nc // ns) + turn, s * nc + z))
        parts.append(lax.ppermute(payload, ("space", "chan"), pairs))
    return parts


def transpose_kernel(cuts, fields_ref, *out_refs):
    fields = fields_ref[...].astype(jnp.float32)
    for plane in range(fields_ref.shape[1]):
        turned = fields[:, plane, :].T.astype(fields_ref.dtype)
        for out_ref, low, high in zip(out_refs, cuts, cuts[1:]):
            out_ref[plane] = turned[low * NZ : high * NZ]


def by_cell(fields, cuts):
    count, depth, _ = fields.shape
    return pl.pallas_call(
        functools.partial(transpose_kernel, cuts),
        out_shape=[
            jax.ShapeDtypeStruct((depth, (high - low) * NZ, count), fields.dtype)
            for low, high in zip(cuts, cuts[1:])
        ],
        in_specs=[IN_VMEM],
        out_specs=[IN_VMEM] * (len(cuts) - 1),
        compiler_params=pltpu.CompilerParams(vmem_limit_bytes=VMEM_LIMIT // 2),
        name="by_cell",
    )(fields)


def hold_kernel(block_ref, weight_ref, token_ref):
    token_ref[...] = jnp.zeros(token_ref.shape, token_ref.dtype)


def hold(block, weights):
    return pl.pallas_call(
        hold_kernel,
        out_shape=jax.ShapeDtypeStruct((8, 128), jnp.float32),
        in_specs=[pl.BlockSpec(memory_space=pl.ANY), IN_VMEM],
        out_specs=IN_VMEM,
        compiler_params=pltpu.CompilerParams(vmem_limit_bytes=VMEM_LIMIT // 2),
        name="hold",
    )(block, weights)


def shifted(value, step):
    rows = value.shape[0]
    z = lax.broadcasted_iota(jnp.int32, value.shape, 0) % NZ
    inside = (z != NZ - 1) if step > 0 else (z != 0)
    rolled = pltpu.roll(value.astype(jnp.float32), (-step) % rows, 0)
    return jnp.where(inside, rolled, 0.0).astype(value.dtype)


def fill_window(plan, part_refs, window_ref):
    ns, nc, cuts, index = plan
    repeats = nc // ns
    low, high = cuts[index], cuts[index + 1]
    first = max(low - 1, 0)
    last = high if high == NY else high - 1
    top = first - 1
    depth = (window_ref.shape[0] - 2) // ns
    count = part_refs[0].shape[2]
    taken = repeats * count
    planes = ns * depth
    chan = lax.axis_index("chan")
    zeros = jnp.zeros(window_ref.shape[1:], window_ref.dtype)
    window_ref[0] = zeros
    window_ref[planes + 1] = zeros
    edge = jnp.zeros((planes, NZ, window_ref.shape[2]), window_ref.dtype)
    if top < 0:
        window_ref[1 : planes + 1, 0:NZ, :] = edge
    if last == NY:
        window_ref[1 : planes + 1, (NY - top) * NZ : (NY - top + 1) * NZ, :] = edge

    def put(values, row, plane, turn):
        rows = values.shape[0]
        for step in range(3):
            piece = values if step == 1 else shifted(values, step - 1)
            for slot in range(repeats):
                begin = step * taken + slot * count

                def store():
                    window_ref[
                        plane, (row - top) * NZ : (row - top) * NZ + rows, begin : begin + count
                    ] = piece

                if repeats == 1:
                    store()
                else:
                    pl.when(turn == slot)(store)

    count_new = rounds_of(index, nc)
    sets = [(index, part_refs[-count_new:])]
    if index:
        sets.append((index - 1, part_refs[:-count_new]))
    for index_of, refs in sets:
        skipped = max(top - cuts[index_of], 0)
        for round_index, part_ref in enumerate(refs):
            source, turn = sender(index_of, chan, round_index, ns, nc)
            begin = (source // 2 * 2 if paired(index_of) else source) * depth
            for plane in range(part_ref.shape[0]):
                put(
                    part_ref[plane, skipped * NZ :, :],
                    cuts[index_of] + skipped,
                    1 + begin + plane,
                    turn,
                )


def add_up(plan, far, cores, weight_ref, window_ref, out_refs):
    ns, nc, cuts, index = plan
    depth = (window_ref.shape[0] - 2) // ns
    cells = window_ref.shape[1] - 2 * NZ
    space = lax.axis_index("space")
    groups = ns // 4
    for order in range(groups):
        mask = 2 * (groups - 1 - order + (groups if far else 0))
        total = None
        for pair in range(9):
            a, b = divmod(pair, 3)
            left = jnp.concatenate(
                [
                    window_ref[
                        pl.ds(depth * (space ^ (mask + core)) + a, depth),
                        b * NZ : b * NZ + cells,
                        :,
                    ].reshape(depth * cells, -1)
                    for core in cores
                ],
                axis=0,
            )
            right = jnp.concatenate([weight_ref[3 * pair + c] for c in range(3)], axis=1)
            product = lax.dot_general(
                left, right, (((1,), (1,)), ((), ())), preferred_element_type=jnp.float32
            )
            total = product if total is None else total + product
        begin, rows = HEAD + order * depth * cells, depth * cells
        for at, ref in enumerate(out_refs):
            ref[begin : begin + rows] = total[at * rows : (at + 1) * rows]
    for ref in out_refs:
        peak = jnp.max(jnp.abs(ref[HEAD:]), axis=0, keepdims=True)
        ref[:HEAD] = jnp.broadcast_to(peak, (HEAD, ref.shape[1]))


def first_kernel(plan, jobs, token_ref, weight_ref, *refs):
    *refs, window_ref = refs
    count = sum(len(cores) for _, cores in jobs)
    part_refs, out_refs = refs[:-count], refs[-count:]
    fill_window(plan, part_refs, window_ref)
    for far, cores in jobs:
        add_up(plan, far, cores, weight_ref, window_ref, out_refs[: len(cores)])
        out_refs = out_refs[len(cores) :]


def later_kernel(plan, jobs, token_ref, weight_ref, window_ref, *out_refs):
    for far, cores in jobs:
        add_up(plan, far, cores, weight_ref, window_ref, out_refs[: len(cores)])
        out_refs = out_refs[len(cores) :]


def partial_sums(token, older, newer, weights, depth, plan, at_once):
    ns, nc, cuts, index = plan
    low, high = cuts[index], cuts[index + 1]
    first = max(low - 1, 0)
    last = high if high == NY else high - 1
    owned, taken = weights.shape[1:]
    cells = (last - first) * NZ
    sums = jax.ShapeDtypeStruct((HEAD + ns // 4 * depth * cells, owned), jnp.float32)
    window = (ns * depth + 2, cells + 2 * NZ, 3 * taken)

    def call(kernel, jobs, inputs, out_shape, scratch_shapes, token=token):
        return pl.pallas_call(
            functools.partial(kernel, plan, jobs),
            out_shape=out_shape,
            in_specs=[pl.BlockSpec(memory_space=pl.ANY)] + [IN_VMEM] * (1 + len(inputs)),
            out_specs=[IN_VMEM] * len(out_shape),
            scratch_shapes=scratch_shapes,
            compiler_params=pltpu.CompilerParams(vmem_limit_bytes=VMEM_LIMIT),
            cost_estimate=pl.CostEstimate(
                flops=27 * 2 * sum(len(cores) for _, cores in jobs) * ns // 4 * depth * cells * owned * taken,
                bytes_accessed=2 * weights.size,
                transcendentals=0,
            ),
            name="partial_sums",
        )(token, weights, *inputs)

    parts = [*older, *newer]
    if at_once:
        jobs = [(True, (1, 0)), (False, (1, 0))]
        far_mate, far_keep, near_mate, near_keep = call(
            first_kernel, jobs, parts, [sums] * 4, [pltpu.VMEM(window, weights.dtype)]
        )
        return far_mate, far_keep, near_mate, lambda token: near_keep
    results = []
    for jobs in STEPS[:-1]:
        count = sum(len(cores) for _, cores in jobs)
        if not results:
            filled = jax.ShapeDtypeStruct(window, weights.dtype)
            *results, filled = call(first_kernel, jobs, parts, [sums] * count + [filled], [])
        else:
            results += call(later_kernel, jobs, [filled], [sums] * count, [])

    def last(token):
        return call(later_kernel, STEPS[-1], [filled], [sums], [], token)[0]

    return *results, last


def finish_kernel(counts, *refs):
    *refs, out_ref, turned_ref = refs
    at = begin = 0
    for count in counts:
        pieces = refs[at : at + count]
        at += count
        cells = pieces[0].shape[0] // out_ref.shape[1]
        for plane in range(out_ref.shape[1]):
            total = pieces[0][plane * cells : (plane + 1) * cells]
            for piece in pieces[1:]:
                total = total + piece[plane * cells : (plane + 1) * cells]
            turned_ref[:, plane, begin : begin + cells] = total.T
        begin += cells
    out_ref[...] = turned_ref[...].astype(out_ref.dtype)


def finish(groups, depth, dtype):
    owned = groups[0][0].shape[1]
    cells = sum(pieces[0].shape[0] for pieces in groups) // depth
    flat = [piece for pieces in groups for piece in pieces]
    return pl.pallas_call(
        functools.partial(finish_kernel, [len(pieces) for pieces in groups]),
        out_shape=jax.ShapeDtypeStruct((owned, depth, cells), dtype),
        in_specs=[IN_VMEM] * len(flat),
        out_specs=IN_VMEM,
        scratch_shapes=[pltpu.VMEM((owned, depth, cells), jnp.float32)],
        compiler_params=pltpu.CompilerParams(vmem_limit_bytes=VMEM_LIMIT // 2),
        name="finish",
    )(*flat)


def level(head):
    exponent, fraction = head[:1].astype(jnp.float32), head[HEAD // 2 : HEAD // 2 + 1]
    return fraction.astype(jnp.float32) * jnp.exp2(exponent)


def coded(sums):
    bound = jnp.maximum(sums[:HEAD], 1e-30)
    exponent = jnp.floor(jnp.log2(bound))
    fraction = bound * jnp.exp2(-exponent) * (1 + 2.0**-10)
    row = lax.broadcasted_iota(jnp.int32, bound.shape, 0)
    head = jnp.where(row < HEAD // 2, exponent, fraction).astype(jnp.float16)
    values = sums[HEAD:]
    power = jnp.exp2(jnp.minimum(jnp.abs(values) / level(head), 1.0) * SPAN - LOWEST)
    return jnp.concatenate([head, jnp.where(values < 0, -power, power).astype(jnp.float16)])


def decoded(sent):
    values = sent[HEAD:].astype(jnp.float32)
    size = (jnp.log2(jnp.abs(values)) + LOWEST) * (level(sent[:HEAD]) / SPAN)
    return jnp.where(values < 0, -size, size)


def swapped(value, bit, ns):
    return lax.ppermute(value, "space", [(i, i ^ (1 << bit)) for i in range(ns)])


def local(fields, conv_weight):
    ns, nc = lax.axis_size("space"), lax.axis_size("chan")
    repeats = nc // ns
    bits = bit_count(ns)
    depth = fields.shape[1]
    blocks = by_cell(fields, CUTS)
    token = hold(blocks[0], conv_weight)
    received = [sent_parts(block, index, ns, nc) for index, block in enumerate(blocks)]
    groups = []
    for index, newer in enumerate(received):
        older = received[index - 1] if index else []
        plan = (ns, nc, CUTS, index)
        far_mate, far_keep, near_mate, last = partial_sums(
            token, older, newer, conv_weight, depth, plan, index == 0
        )
        token, far_mate = lax.optimization_barrier((token, far_mate))
        far, after = far_keep + swapped(far_mate, 0, ns), token
        if bits == 2:
            sent = coded(far)
            after, sent = lax.optimization_barrier((token, sent))
        near = last(after) + swapped(near_mate, 0, ns)
        for bit in range(bits - 1, 1, -1):
            total = near + swapped(far, bit, ns)
            middle = HEAD + (total.shape[0] - HEAD) // 2
            far, near = total[:middle], jnp.concatenate([total[:HEAD], total[middle:]])
        if bits > 2:
            sent = coded(far)
        groups.append([near[HEAD:], decoded(swapped(sent, 1, ns))])
    return finish(groups, fields.shape[1], fields.dtype)


def solution(mesh):
    return jax.shard_map(
        local,
        mesh=mesh,
        in_specs=(P("chan", ("groups", "space"), None), P(None, "chan", "space")),
        out_specs=P("chan", ("groups", "space"), None),
        check_vma=False,
    )
```

```python
import functools

import jax
import jax.numpy as jnp
from jax import lax
from jax.experimental import pallas as pl
from jax.experimental.pallas import tpu as pltpu
from jax.sharding import PartitionSpec as P

NY = 16
NZ = 16
CUTS = (0, 9, 16)
STEPS = [[(True, (1,))], [(True, (0,)), (False, (1,))], [(False, (0,))]]
HEAD = 16
LOWEST, SPAN = 14.0, 29.0
VMEM_LIMIT = 16 * 2**20
IN_VMEM = pl.BlockSpec(memory_space=pltpu.VMEM)


def bit_count(n):
    return n.bit_length() - 1


def reversed_bits(value, bits):
    out = 0
    for bit in range(bits):
        out = out | (((value >> bit) & 1) << (bits - 1 - bit))
    return out


def paired(index):
    return index >= 0


def rounds_of(index, nc):
    return nc // 2 if paired(index) else nc


def sender(index, chan, round_index, ns, nc):
    masks = ns // 2 if paired(index) else ns
    mask, jump = round_index % masks, round_index // masks
    source = reversed_bits(chan % ns, bit_count(ns)) ^ (2 * mask if paired(index) else mask)
    return source, (jump + chan // ns) % (nc // ns)


def pair_kernel(own_ref, mate_ref, out_ref):
    depth = own_ref.shape[0]
    core = lax.axis_index("space") % 2
    out_ref[pl.ds(depth * core, depth)] = own_ref[...]
    out_ref[pl.ds(depth * (1 - core), depth)] = mate_ref[...]


def pair(own, mate):
    depth, cells, count = own.shape
    return pl.pallas_call(
        pair_kernel,
        out_shape=jax.ShapeDtypeStruct((2 * depth, cells, count), own.dtype),
        in_specs=[IN_VMEM] * 2,
        out_specs=IN_VMEM,
        compiler_params=pltpu.CompilerParams(vmem_limit_bytes=VMEM_LIMIT // 2),
        name="pair",
    )(own, mate)


def sent_parts(block, index, ns, nc):
    payload = pair(block, swapped(block, 0, ns)) if paired(index) else block
    parts = []
    for round_index in range(rounds_of(index, nc)):
        pairs = []
        for s in range(ns):
            for z in range(nc):
                source, turn = sender(index, z, round_index, ns, nc)
                pairs.append((source * nc + s * (nc // ns) + turn, s * nc + z))
        parts.append(lax.ppermute(payload, ("space", "chan"), pairs))
    return parts


def transpose_kernel(cuts, fields_ref, *out_refs):
    fields = fields_ref[...].astype(jnp.float32)
    for plane in range(fields_ref.shape[1]):
        turned = fields[:, plane, :].T.astype(fields_ref.dtype)
        for out_ref, low, high in zip(out_refs, cuts, cuts[1:]):
            out_ref[plane] = turned[low * NZ : high * NZ]


def by_cell(fields, cuts):
    count, depth, _ = fields.shape
    return pl.pallas_call(
        functools.partial(transpose_kernel, cuts),
        out_shape=[
            jax.ShapeDtypeStruct((depth, (high - low) * NZ, count), fields.dtype)
            for low, high in zip(cuts, cuts[1:])
        ],
        in_specs=[IN_VMEM],
        out_specs=[IN_VMEM] * (len(cuts) - 1),
        compiler_params=pltpu.CompilerParams(vmem_limit_bytes=VMEM_LIMIT // 2),
        name="by_cell",
    )(fields)


def hold_kernel(block_ref, weight_ref, token_ref):
    token_ref[...] = jnp.zeros(token_ref.shape, token_ref.dtype)


def hold(block, weights):
    return pl.pallas_call(
        hold_kernel,
        out_shape=jax.ShapeDtypeStruct((8, 128), jnp.float32),
        in_specs=[pl.BlockSpec(memory_space=pl.ANY), IN_VMEM],
        out_specs=IN_VMEM,
        compiler_params=pltpu.CompilerParams(vmem_limit_bytes=VMEM_LIMIT // 2),
        name="hold",
    )(block, weights)


def shifted(value, step):
    rows = value.shape[0]
    z = lax.broadcasted_iota(jnp.int32, value.shape, 0) % NZ
    inside = (z != NZ - 1) if step > 0 else (z != 0)
    rolled = pltpu.roll(value.astype(jnp.float32), (-step) % rows, 0)
    return jnp.where(inside, rolled, 0.0).astype(value.dtype)


def fill_window(plan, part_refs, window_ref):
    ns, nc, cuts, index = plan
    repeats = nc // ns
    low, high = cuts[index], cuts[index + 1]
    first = max(low - 1, 0)
    last = high if high == NY else high - 1
    top = first - 1
    depth = (window_ref.shape[0] - 2) // ns
    count = part_refs[0].shape[2]
    taken = repeats * count
    planes = ns * depth
    chan = lax.axis_index("chan")
    zeros = jnp.zeros(window_ref.shape[1:], window_ref.dtype)
    window_ref[0] = zeros
    window_ref[planes + 1] = zeros
    edge = jnp.zeros((planes, NZ, window_ref.shape[2]), window_ref.dtype)
    if top < 0:
        window_ref[1 : planes + 1, 0:NZ, :] = edge
    if last == NY:
        window_ref[1 : planes + 1, (NY - top) * NZ : (NY - top + 1) * NZ, :] = edge

    def put(values, row, plane, turn):
        rows = values.shape[0]
        for step in range(3):
            piece = values if step == 1 else shifted(values, step - 1)
            for slot in range(repeats):
                begin = step * taken + slot * count

                def store():
                    window_ref[
                        plane, (row - top) * NZ : (row - top) * NZ + rows, begin : begin + count
                    ] = piece

                if repeats == 1:
                    store()
                else:
                    pl.when(turn == slot)(store)

    count_new = rounds_of(index, nc)
    sets = [(index, part_refs[-count_new:])]
    if index:
        sets.append((index - 1, part_refs[:-count_new]))
    for index_of, refs in sets:
        skipped = max(top - cuts[index_of], 0)
        for round_index, part_ref in enumerate(refs):
            source, turn = sender(index_of, chan, round_index, ns, nc)
            begin = (source // 2 * 2 if paired(index_of) else source) * depth
            for plane in range(part_ref.shape[0]):
                put(
                    part_ref[plane, skipped * NZ :, :],
                    cuts[index_of] + skipped,
                    1 + begin + plane,
                    turn,
                )


def add_up(plan, far, cores, weight_ref, window_ref, out_refs):
    ns, nc, cuts, index = plan
    depth = (window_ref.shape[0] - 2) // ns
    cells = window_ref.shape[1] - 2 * NZ
    space = lax.axis_index("space")
    groups = ns // 4
    for order in range(groups):
        mask = 2 * (groups - 1 - order + (groups if far else 0))
        total = None
        for pair in range(9):
            a, b = divmod(pair, 3)
            left = jnp.concatenate(
                [
                    window_ref[
                        pl.ds(depth * (space ^ (mask + core)) + a, depth),
                        b * NZ : b * NZ + cells,
                        :,
                    ].reshape(depth * cells, -1)
                    for core in cores
                ],
                axis=0,
            )
            right = jnp.concatenate([weight_ref[3 * pair + c] for c in range(3)], axis=1)
            product = lax.dot_general(
                left, right, (((1,), (1,)), ((), ())), preferred_element_type=jnp.float32
            )
            total = product if total is None else total + product
        begin, rows = HEAD + order * depth * cells, depth * cells
        for at, ref in enumerate(out_refs):
            ref[begin : begin + rows] = total[at * rows : (at + 1) * rows]
    for ref in out_refs:
        peak = jnp.max(jnp.abs(ref[HEAD:]), axis=0, keepdims=True)
        ref[:HEAD] = jnp.broadcast_to(peak, (HEAD, ref.shape[1]))


def first_kernel(plan, jobs, token_ref, weight_ref, *refs):
    *refs, window_ref = refs
    count = sum(len(cores) for _, cores in jobs)
    part_refs, out_refs = refs[:-count], refs[-count:]
    fill_window(plan, part_refs, window_ref)
    for far, cores in jobs:
        add_up(plan, far, cores, weight_ref, window_ref, out_refs[: len(cores)])
        out_refs = out_refs[len(cores) :]


def later_kernel(plan, jobs, token_ref, weight_ref, window_ref, *out_refs):
    for far, cores in jobs:
        add_up(plan, far, cores, weight_ref, window_ref, out_refs[: len(cores)])
        out_refs = out_refs[len(cores) :]


def partial_sums(token, older, newer, weights, depth, plan, at_once):
    ns, nc, cuts, index = plan
    low, high = cuts[index], cuts[index + 1]
    first = max(low - 1, 0)
    last = high if high == NY else high - 1
    owned, taken = weights.shape[1:]
    cells = (last - first) * NZ
    sums = jax.ShapeDtypeStruct((HEAD + ns // 4 * depth * cells, owned), jnp.float32)
    window = (ns * depth + 2, cells + 2 * NZ, 3 * taken)

    def call(kernel, jobs, inputs, out_shape, scratch_shapes, token=token):
        return pl.pallas_call(
            functools.partial(kernel, plan, jobs),
            out_shape=out_shape,
            in_specs=[pl.BlockSpec(memory_space=pl.ANY)] + [IN_VMEM] * (1 + len(inputs)),
            out_specs=[IN_VMEM] * len(out_shape),
            scratch_shapes=scratch_shapes,
            compiler_params=pltpu.CompilerParams(vmem_limit_bytes=VMEM_LIMIT),
            cost_estimate=pl.CostEstimate(
                flops=27 * 2 * sum(len(cores) for _, cores in jobs) * ns // 4 * depth * cells * owned * taken,
                bytes_accessed=2 * weights.size,
                transcendentals=0,
            ),
            name="partial_sums",
        )(token, weights, *inputs)

    parts = [*older, *newer]
    if at_once:
        jobs = [(True, (1, 0)), (False, (1, 0))]
        far_mate, far_keep, near_mate, near_keep = call(
            first_kernel, jobs, parts, [sums] * 4, [pltpu.VMEM(window, weights.dtype)]
        )
        return far_mate, far_keep, near_mate, lambda token: near_keep
    results = []
    for jobs in STEPS[:-1]:
        count = sum(len(cores) for _, cores in jobs)
        if not results:
            filled = jax.ShapeDtypeStruct(window, weights.dtype)
            *results, filled = call(first_kernel, jobs, parts, [sums] * count + [filled], [])
        else:
            results += call(later_kernel, jobs, [filled], [sums] * count, [])

    def last(token):
        return call(later_kernel, STEPS[-1], [filled], [sums], [], token)[0]

    return *results, last


def finish_kernel(counts, *refs):
    *refs, out_ref, turned_ref = refs
    at = begin = 0
    for count in counts:
        pieces = refs[at : at + count]
        at += count
        cells = pieces[0].shape[0] // out_ref.shape[1]
        for plane in range(out_ref.shape[1]):
            total = pieces[0][plane * cells : (plane + 1) * cells]
            for piece in pieces[1:]:
                total = total + piece[plane * cells : (plane + 1) * cells]
            turned_ref[:, plane, begin : begin + cells] = total.T
        begin += cells
    out_ref[...] = turned_ref[...].astype(out_ref.dtype)


def finish(groups, depth, dtype):
    owned = groups[0][0].shape[1]
    cells = sum(pieces[0].shape[0] for pieces in groups) // depth
    flat = [piece for pieces in groups for piece in pieces]
    return pl.pallas_call(
        functools.partial(finish_kernel, [len(pieces) for pieces in groups]),
        out_shape=jax.ShapeDtypeStruct((owned, depth, cells), dtype),
        in_specs=[IN_VMEM] * len(flat),
        out_specs=IN_VMEM,
        scratch_shapes=[pltpu.VMEM((owned, depth, cells), jnp.float32)],
        compiler_params=pltpu.CompilerParams(vmem_limit_bytes=VMEM_LIMIT // 2),
        name="finish",
    )(*flat)


def level(head):
    exponent, fraction = head[:1].astype(jnp.float32), head[HEAD // 2 : HEAD // 2 + 1]
    return fraction.astype(jnp.float32) * jnp.exp2(exponent)


def coded(sums):
    bound = jnp.maximum(sums[:HEAD], 1e-30)
    exponent = jnp.floor(jnp.log2(bound))
    fraction = bound * jnp.exp2(-exponent) * (1 + 2.0**-10)
    row = lax.broadcasted_iota(jnp.int32, bound.shape, 0)
    head = jnp.where(row < HEAD // 2, exponent, fraction).astype(jnp.float16)
    values = sums[HEAD:]
    power = jnp.exp2(jnp.minimum(jnp.abs(values) / level(head), 1.0) * SPAN - LOWEST)
    return jnp.concatenate([head, jnp.where(values < 0, -power, power).astype(jnp.float16)])


def decoded(sent):
    values = sent[HEAD:].astype(jnp.float32)
    size = (jnp.log2(jnp.abs(values)) + LOWEST) * (level(sent[:HEAD]) / SPAN)
    return jnp.where(values < 0, -size, size)


def swapped(value, bit, ns):
    return lax.ppermute(value, "space", [(i, i ^ (1 << bit)) for i in range(ns)])


def local(fields, conv_weight):
    ns, nc = lax.axis_size("space"), lax.axis_size("chan")
    repeats = nc // ns
    bits = bit_count(ns)
    depth = fields.shape[1]
    blocks = by_cell(fields, CUTS)
    token = hold(blocks[0], conv_weight)
    received = [sent_parts(block, index, ns, nc) for index, block in enumerate(blocks)]
    groups = []
    for index, newer in enumerate(received):
        older = received[index - 1] if index else []
        plan = (ns, nc, CUTS, index)
        far_mate, far_keep, near_mate, last = partial_sums(
            token, older, newer, conv_weight, depth, plan, index == 0
        )
        token, far_mate = lax.optimization_barrier((token, far_mate))
        far, after = far_keep + swapped(far_mate, 0, ns), token
        if bits == 2:
            sent = coded(far)
            after, sent = lax.optimization_barrier((token, sent))
        near = last(after) + swapped(near_mate, 0, ns)
        for bit in range(bits - 1, 1, -1):
            total = near + swapped(far, bit, ns)
            middle = HEAD + (total.shape[0] - HEAD) // 2
            far, near = total[:middle], jnp.concatenate([total[:HEAD], total[middle:]])
        if bits > 2:
            sent = coded(far)
        groups.append([near[HEAD:], decoded(swapped(sent, 1, ns))])
    return finish(groups, fields.shape[1], fields.dtype)


def solution(mesh):
    return jax.shard_map(
        local,
        mesh=mesh,
        in_specs=(P("chan", ("groups", "space"), None), P(None, "chan", "space")),
        out_specs=P("chan", ("groups", "space"), None),
        check_vma=False,
    )
```
